32 devices in a mesh: expert: 16 (over z, x, core), mp: 2 (over y).
Axes of the slice: x: 2, y: 2, z: 4, core: 2. Of those that a mesh axis runs over, the one named last changes fastest.
Arguments:
- routes: int32 [4096], P('expert'), may hold values from 0 to 15
- slots: int32 [4096], P('expert'), may hold values from -1 to 19, as said below
- gate: float32 [4096], P('expert'), may hold values from 0.2 to 1
- grad_out: bfloat16 [4096, 4096], P('expert', 'mp'), may hold values from -6 to 6
- saved_inputs: bfloat16 [16, 320, 4096], P('expert'), may hold values from -6 to 6
- w_in: bfloat16 [16, 4096, 5120], P('expert', None, 'mp'), may hold values from -0.09375 to 0.09375
- w_out: bfloat16 [16, 5120, 4096], P('expert', 'mp'), may hold values from -0.078125 to 0.078125
- dense_partial: float32 [16, 256, 4096], P('expert', None, 'mp'), may hold values from -6 to 6
Outputs:
- grad_in: bfloat16 [4096, 4096], P('expert', 'mp')
- dense_sum: float32 [256, 4096], P(None, 'mp')
The draws below stay inside these ranges and needn't reach their ends.
Inputs may be any that keep to these rules, and one draw needn't show every extreme that they name: Within each group, the tokens routed to one expert take slots 0, 1, 2, ... in token order; the k-th such token has slot k - 1 if k <= 20, else -1.
All inputs are finite; a program needn't handle non-finite values.
Results may differ from the reference program's by a relative error of at most 0.0058.
Values may be sent and summed in bfloat16 or wider, within the bound.
No kernel may reach another device: no remote copies, remote signals or barrier semaphores. Data moves between devices by JAX's collectives and lax.ppermute only.
A program may use at most 128 MiB of HBM per device.

```python
import math
import jax
import jax.numpy as jnp
from jax import lax

D = 4096
FF = 5120
TOK_GRP = 256
BROWS = 256
EXPERTS = 16
GROUPS = 16
TOKENS = 4096
CAP = 20
ROWS = 320


def routing(source_key):
    groups = TOKENS // TOK_GRP
    capacity = 5 * TOK_GRP // (4 * EXPERTS)
    hot_key, pick_key, order_key = jax.random.split(source_key, 3)
    hot_expert = jax.random.randint(hot_key, (), 0, EXPERTS)
    uniform_pick = jax.random.randint(pick_key, (groups, TOK_GRP), 0, EXPERTS)
    order_rank = jax.vmap(lambda subkey: jax.random.permutation(subkey, TOK_GRP))(jax.random.split(order_key, groups))
    chosen = jnp.where(order_rank <= capacity, hot_expert, uniform_pick).astype(jnp.int32)
    onehot = (chosen[:, :, None] == jnp.arange(EXPERTS, dtype=jnp.int32)[None, None, :]).astype(jnp.int32)
    before = jnp.cumsum(onehot, axis=1) - onehot
    placed = jnp.sum(before * onehot, axis=2)
    placed = jnp.where(placed < capacity, placed, -1).astype(jnp.int32)
    return (chosen.reshape(-1), placed.reshape(-1))


def draw_routes(key, part):
    return routing(key)[0]


def draw_slots(key, part):
    return routing(key)[1]


def level_of(own_key, dims, cuts, least, top_value):
    factor_of = 1.0
    for dim, blocks in cuts:
        heights = jax.random.uniform(jax.random.fold_in(jax.random.fold_in(own_key, 6), dim), (blocks,), jnp.float32, least / len(cuts), top_value / len(cuts))
        factor_of = factor_of * jnp.repeat(jnp.exp(heights), dims[dim] // blocks).reshape((-1,) + (1,) * (len(dims) - 1 - dim))
    return factor_of


def scatter_about(key, extent, width, limit, pieces=(), held_as=jnp.bfloat16):
    loudness = level_of(key, extent, pieces, -0.22, 0.18) if pieces else 1.0
    array = jax.random.normal(key, extent, jnp.float32) * width * loudness
    return jnp.minimum(jnp.maximum(array, -limit), limit).astype(held_as)


def setup_inputs(seed: int = 0) -> dict:
    arg_keys = jax.random.split(jax.random.key(seed), 9)
    return {
        "routes": draw_routes(jax.random.fold_in(arg_keys[8], 71), 0),
        "slots": draw_slots(jax.random.fold_in(arg_keys[8], 71), 0),
        "gate": jnp.clip(0.2 + 0.8 * jax.random.uniform(arg_keys[2], (TOKENS,), jnp.float32) ** level_of(arg_keys[2], (TOKENS,), ((0, 16),), -0.2, 0.2), 0.2, 1.0),
        "grad_out": scatter_about(arg_keys[3], (TOKENS, D), 1.0, 6.0, ((0, 16), (1, 2))),
        "saved_inputs": scatter_about(arg_keys[4], (EXPERTS, ROWS, D), 1.0, 6.0, ((0, 16),)),
        "w_in": scatter_about(arg_keys[5], (EXPERTS, D, FF), D ** -0.5, 0.09375, ((0, 16), (2, 2))),
        "w_out": scatter_about(arg_keys[6], (EXPERTS, FF, D), FF ** -0.5, 0.078125, ((0, 16), (1, 2))),
        "dense_partial": scatter_about(arg_keys[7], (GROUPS, BROWS, D), 1.0, 6.0, ((0, 16), (2, 2)), jnp.float32),
    }


gelu_scale = math.sqrt(2.0 / math.pi)
cubic_coef = 0.044715

def slope_of(preact):
    inner = gelu_scale * (preact + cubic_coef * preact * preact * preact)
    tanh_val = jnp.tanh(inner)
    return 0.5 * (1.0 + tanh_val) + 0.5 * preact * (1.0 - tanh_val * tanh_val) * gelu_scale * (1.0 + 3.0 * cubic_coef * preact * preact)

def expert_pass(members):
    inputs, grad_rows, w_first, w_second = members
    preact = jnp.dot(inputs, w_first, preferred_element_type=jnp.float32)
    upstream = lax.dot_general(grad_rows, w_second, (((1,), (1,)), ((), ())), preferred_element_type=jnp.float32)
    hidden_grad = (upstream * slope_of(preact)).astype(jnp.bfloat16)
    result = lax.dot_general(hidden_grad, w_first, (((1,), (1,)), ((), ())), preferred_element_type=jnp.float32)
    return result.astype(jnp.bfloat16)

def reference(routes, slots, gate, grad_out, saved_inputs, w_in, w_out, dense_partial):
    group_of = (jnp.arange(TOKENS) // TOK_GRP).astype(jnp.int32)
    overall = EXPERTS * ROWS
    position = routes.astype(jnp.int32) * ROWS + group_of * CAP + slots.astype(jnp.int32)
    position = jnp.where(slots >= 0, position, overall).astype(jnp.int32)
    scaled = (gate[:, None] * grad_out.astype(jnp.float32)).astype(jnp.bfloat16)
    dispatched = jnp.zeros((overall, D), jnp.bfloat16).at[position].set(scaled, mode='drop')
    dispatched = dispatched.reshape(EXPERTS, ROWS, D)
    returned = lax.map(expert_pass, (saved_inputs, dispatched, w_in, w_out)).reshape(overall, D)
    picked = jnp.take(returned, jnp.minimum(position, overall - 1).astype(jnp.int32), axis=0)
    grad_in = jnp.where((slots >= 0)[:, None], picked, jnp.zeros_like(picked))
    dense_sum = lax.optimization_barrier(jnp.sum(dense_partial, axis=0))
    return (grad_in, dense_sum)
```

```python
import math

import jax
import jax.numpy as jnp
from jax import lax
from jax.sharding import PartitionSpec as P

gelu_scale = math.sqrt(2.0 / math.pi)
cubic_coef = 0.044715
BF16 = jnp.bfloat16
F32 = jnp.float32
NT = (((1,), (1,)), ((), ()))


def slope_of(preact):
    inner = gelu_scale * (preact + cubic_coef * preact * preact * preact)
    tanh_val = jnp.tanh(inner)
    return 0.5 * (1.0 + tanh_val) + 0.5 * preact * (1.0 - tanh_val * tanh_val) * gelu_scale * (
        1.0 + 3.0 * cubic_coef * preact * preact
    )


def after(value, *others):
    return lax.optimization_barrier((value,) + others)[0]


def xor_send(value, axis, bit):
    size = lax.axis_size(axis)
    return lax.ppermute(value, axis, [(i, i ^ bit) for i in range(size)])


def halve(mine, axis, bit):
    rows = mine.shape[0] // 2
    upper = (lax.axis_index(axis) & bit) != 0
    kept = jnp.where(upper, mine[rows:], mine[:rows])
    sent = jnp.where(upper, mine[:rows], mine[rows:])
    return kept + xor_send(sent.astype(BF16), axis, bit).astype(F32)


def double(mine, axis, bit):
    upper = (lax.axis_index(axis) & bit) != 0
    other = xor_send(mine, axis, bit)
    return jnp.concatenate([jnp.where(upper, other, mine), jnp.where(upper, mine, other)], axis=0)


def bits_of(size):
    return [1 << i for i in range(size.bit_length() - 1)]


def summed_over(part, axis):
    bits = bits_of(lax.axis_size(axis))
    for bit in bits:
        part = halve(part, axis, bit)
    part = part.astype(BF16)
    for bit in reversed(bits):
        part = double(part, axis, bit)
    return part.astype(F32)


def one_hot(rows, columns):
    return (lax.broadcasted_iota(jnp.int32, (rows, columns.shape[0]), 0) == columns[None, :]).astype(BF16)


def dot(a, b):
    return jnp.dot(a, b, preferred_element_type=F32)


def chunk_widths(features, share):
    unit = 256
    if features % unit or features < 2 * unit:
        return [features]
    first = int(round(features * share / unit)) * unit
    return [first, features - first]


def on_device(routes, slots, gate, grad_out, saved_inputs, w_in, w_out, dense_partial):
    groups = lax.axis_size("expert")
    models = lax.axis_size("mp")
    me = lax.axis_index("mp")
    slot_rows = saved_inputs.shape[1]
    cap = slot_rows // groups
    tok_count, features = grad_out.shape
    pair = models == 2
    fold = 2 if pair and features % 512 == 0 else 1
    rows = fold * slot_rows

    dense_sum = summed_over(dense_partial[0], "expert")

    scaled = (gate[:, None] * grad_out.astype(F32)).astype(BF16)
    columns = jnp.concatenate(
        [jnp.where(slots >= 0, routes * (fold * cap) + h * cap + slots, -1) for h in range(fold)]
    )
    table = one_hot(rows, columns)
    slot = jnp.arange(slot_rows, dtype=jnp.int32)
    spread = [one_hot(rows, (slot // cap) * (fold * cap) + h * cap + slot % cap) for h in range(fold)]

    widths = chunk_widths(features, 0.625) if pair else [features]
    starts = [sum(widths[:i]) for i in range(len(widths))]

    def all_to_all(block):
        wide = block.shape[1]
        block = block.reshape(groups, fold * cap, wide)
        return lax.all_to_all(block, "expert", split_axis=0, concat_axis=0, tiled=True).reshape(rows, wide)

    mine = []
    for start, width in zip(starts, widths):
        part = width // fold
        stacked = jnp.concatenate(
            [scaled[:, start + h * part : start + (h + 1) * part] for h in range(fold)], axis=0
        )
        arrived = all_to_all(dot(table, stacked).astype(BF16))
        mine.append(
            jnp.concatenate(
                [
                    lax.dot_general(t, arrived, (((0,), (0,)), ((), ())), preferred_element_type=F32).astype(BF16)
                    for t in spread
                ],
                axis=1,
            )
        )

    slopes = slope_of(dot(saved_inputs[0], w_in[0]))

    if pair:
        theirs = [xor_send(x, "mp", 1) for x in mine]
        upstream = None
        for start, width, own, other in zip(starts, widths, mine, theirs):
            for who, x in ((me, own), (1 - me, other)):
                w = lax.dynamic_slice_in_dim(w_out[0], who * features + start, width, 1)
                term = lax.dot_general(x, w, NT, preferred_element_type=F32)
                upstream = term if upstream is None else upstream + term
    else:
        upstream = lax.dot_general(
            lax.all_gather(mine[0], "mp", axis=1, tiled=True), w_out[0], NT, preferred_element_type=F32
        )
    hidden = (upstream * slopes).astype(BF16)

    def share_of(who, start, width):
        w = lax.dynamic_slice_in_dim(w_in[0], who * features + start, width, 0)
        return lax.dot_general(hidden, w, NT, preferred_element_type=F32)

    outs = []
    if pair:
        sent = [
            xor_send(share_of(1 - me, start, width).astype(BF16), "mp", 1)
            for start, width in reversed(list(zip(starts, widths)))
        ][::-1]
    for i, (start, width) in reversed(list(enumerate(zip(starts, widths)))):
        part = width // fold
        if pair:
            total = (share_of(me, start, width) + sent[i].astype(F32)).astype(BF16)
        else:
            total = lax.psum_scatter(
                lax.dot_general(hidden, w_in[0], NT, preferred_element_type=F32),
                "mp",
                scatter_dimension=1,
                tiled=True,
            ).astype(BF16)
        folded = sum(dot(t, total[:, h * part : (h + 1) * part]) for h, t in enumerate(spread))
        back = all_to_all(folded.astype(BF16))
        outs = [
            lax.dot_general(
                table[:, h * tok_count : (h + 1) * tok_count],
                back,
                (((0,), (0,)), ((), ())),
                preferred_element_type=F32,
            ).astype(BF16)
            for h in range(fold)
        ] + outs
    return (jnp.concatenate(outs, axis=1), dense_sum)


def solution(mesh):
    in_specs = (
        P("expert"),
        P("expert"),
        P("expert"),
        P("expert", "mp"),
        P("expert", None, None),
        P("expert", None, "mp"),
        P("expert", "mp", None),
        P("expert", None, "mp"),
    )
    out_specs = (P("expert", "mp"), P(None, "mp"))
    return jax.shard_map(
        on_device, mesh=mesh, in_specs=in_specs, out_specs=out_specs, check_vma=False
    )
```

```python
import math

import jax
import jax.numpy as jnp
from jax import lax
from jax.sharding import PartitionSpec as P

gelu_scale = math.sqrt(2.0 / math.pi)
cubic_coef = 0.044715
BF16 = jnp.bfloat16
F32 = jnp.float32
NT = (((1,), (1,)), ((), ()))


def slope_of(preact):
    inner = gelu_scale * (preact + cubic_coef * preact * preact * preact)
    tanh_val = jnp.tanh(inner)
    return 0.5 * (1.0 + tanh_val) + 0.5 * preact * (1.0 - tanh_val * tanh_val) * gelu_scale * (
        1.0 + 3.0 * cubic_coef * preact * preact
    )


def after(value, *others):
    return lax.optimization_barrier((value,) + others)[0]


def xor_send(value, axis, bit):
    size = lax.axis_size(axis)
    return lax.ppermute(value, axis, [(i, i ^ bit) for i in range(size)])


def halve(mine, axis, bit):
    rows = mine.shape[0] // 2
    upper = (lax.axis_index(axis) & bit) != 0
    kept = jnp.where(upper, mine[rows:], mine[:rows])
    sent = jnp.where(upper, mine[:rows], mine[rows:])
    return kept + xor_send(sent.astype(BF16), axis, bit).astype(F32)


def double(mine, axis, bit):
    upper = (lax.axis_index(axis) & bit) != 0
    other = xor_send(mine, axis, bit)
    return jnp.concatenate([jnp.where(upper, other, mine), jnp.where(upper, mine, other)], axis=0)


def bits_of(size):
    return [1 << i for i in range(size.bit_length() - 1)]


def summed_over(part, axis, early, gate):
    bits = bits_of(lax.axis_size(axis))
    for i, bit in enumerate(bits):
        if i == early:
            part = after(part, gate)
        part = halve(part, axis, bit)
    part = part.astype(BF16)
    for bit in reversed(bits):
        part = double(part, axis, bit)
    return part.astype(F32)


def one_hot(rows, columns):
    return (lax.broadcasted_iota(jnp.int32, (rows, columns.shape[0]), 0) == columns[None, :]).astype(BF16)


def dot(a, b):
    return jnp.dot(a, b, preferred_element_type=F32)


def chunk_widths(features, share):
    unit = 256
    if features % unit or features < 2 * unit:
        return [features]
    first = int(round(features * share / unit)) * unit
    return [first, features - first]


def on_device(routes, slots, gate, grad_out, saved_inputs, w_in, w_out, dense_partial):
    groups = lax.axis_size("expert")
    models = lax.axis_size("mp")
    me = lax.axis_index("mp")
    slot_rows = saved_inputs.shape[1]
    cap = slot_rows // groups
    tok_count, features = grad_out.shape
    pair = models == 2
    fold = 2 if pair and features % 512 == 0 else 1
    rows = fold * slot_rows

    scaled = (gate[:, None] * grad_out.astype(F32)).astype(BF16)
    columns = jnp.concatenate(
        [jnp.where(slots >= 0, routes * (fold * cap) + h * cap + slots, -1) for h in range(fold)]
    )
    table = one_hot(rows, columns)
    slot = jnp.arange(slot_rows, dtype=jnp.int32)
    spread = [one_hot(rows, (slot // cap) * (fold * cap) + h * cap + slot % cap) for h in range(fold)]

    widths = chunk_widths(features, 0.625) if pair else [features]
    starts = [sum(widths[:i]) for i in range(len(widths))]

    def all_to_all(block):
        wide = block.shape[1]
        block = block.reshape(groups, fold * cap, wide)
        return lax.all_to_all(block, "expert", split_axis=0, concat_axis=0, tiled=True).reshape(rows, wide)

    def nt_dot(a, b):
        return lax.dot_general(a, b, NT, preferred_element_type=F32)

    def tn_dot(a, b):
        return lax.dot_general(a, b, (((0,), (0,)), ((), ())), preferred_element_type=F32)

    outgoing = []
    for start, width in zip(starts, widths):
        part = width // fold
        stacked = jnp.concatenate(
            [scaled[:, start + h * part : start + (h + 1) * part] for h in range(fold)], axis=0
        )
        outgoing.append(dot(table, stacked).astype(BF16))

    saved = after(saved_inputs[0], outgoing[0])
    slopes = lax.optimization_barrier(slope_of(dot(saved, w_in[0])))
    arrived = [all_to_all(outgoing[0])]
    for block in outgoing[1:]:
        arrived.append(all_to_all(after(block, arrived[-1], slopes)))
    mine = [jnp.concatenate([tn_dot(t, block).astype(BF16) for t in spread], axis=1) for block in arrived]
    dense_sum = summed_over(after(dense_partial[0], outgoing[0]), "expert", 2, arrived[-1])

    if pair:
        upstream = None
        waiting = []
        for i, (start, width) in enumerate(zip(starts, widths)):
            own = mine[i]
            if upstream is not None:
                own = after(own, upstream)
            theirs = xor_send(own, "mp", 1)
            todo = waiting + [(me, start, width, own)]
            for who, first, wide, x in todo:
                w = lax.dynamic_slice_in_dim(w_out[0], who * features + first, wide, 1)
                term = nt_dot(x, w)
                upstream = lax.optimization_barrier(term if upstream is None else upstream + term)
            waiting = [(1 - me, start, width, theirs)]
        for who, first, wide, x in waiting:
            w = lax.dynamic_slice_in_dim(w_out[0], who * features + first, wide, 1)
            upstream = upstream + nt_dot(x, w)
    else:
        upstream = nt_dot(lax.all_gather(mine[0], "mp", axis=1, tiled=True), w_out[0])
    hidden = lax.optimization_barrier((upstream * slopes).astype(BF16))

    def share_of(who, start, width):
        return nt_dot(hidden, lax.dynamic_slice_in_dim(w_in[0], who * features + start, width, 0))

    order = list(reversed(range(len(widths))))
    if pair:
        sent = {i: xor_send(share_of(1 - me, starts[i], widths[i]).astype(BF16), "mp", 1) for i in order}
        kept = {i: lax.optimization_barrier(share_of(me, starts[i], widths[i])) for i in order}
    outs = {}
    last = None
    for i in order:
        part = widths[i] // fold
        if pair:
            total = (kept[i] + sent[i].astype(F32)).astype(BF16)
        else:
            total = lax.psum_scatter(
                nt_dot(hidden, w_in[0]), "mp", scatter_dimension=1, tiled=True
            ).astype(BF16)
        folded = sum(dot(t, total[:, h * part : (h + 1) * part]) for h, t in enumerate(spread)).astype(BF16)
        if last is not None:
            folded = after(folded, last)
        last = all_to_all(folded)
        outs[i] = jnp.concatenate(
            [tn_dot(table[:, h * tok_count : (h + 1) * tok_count], last).astype(BF16) for h in range(fold)],
            axis=1,
        )
    return (jnp.concatenate([outs[i] for i in sorted(order)], axis=1), dense_sum)


def solution(mesh):
    in_specs = (
        P("expert"),
        P("expert"),
        P("expert"),
        P("expert", "mp"),
        P("expert", None, None),
        P("expert", None, "mp"),
        P("expert", "mp", None),
        P("expert", None, "mp"),
    )
    out_specs = (P("expert", "mp"), P(None, "mp"))
    return jax.shard_map(
        on_device, mesh=mesh, in_specs=in_specs, out_specs=out_specs, check_vma=False
    )
```

```python
import math

import jax
import jax.numpy as jnp
from jax import lax
from jax.sharding import PartitionSpec as P

gelu_scale = math.sqrt(2.0 / math.pi)
cubic_coef = 0.044715
BF16 = jnp.bfloat16
F32 = jnp.float32
NT = (((1,), (1,)), ((), ()))


def slope_of(preact):
    inner = gelu_scale * (preact + cubic_coef * preact * preact * preact)
    tanh_val = jnp.tanh(inner)
    return 0.5 * (1.0 + tanh_val) + 0.5 * preact * (1.0 - tanh_val * tanh_val) * gelu_scale * (
        1.0 + 3.0 * cubic_coef * preact * preact
    )


def after(value, *others):
    return lax.optimization_barrier((value,) + others)[0]


def xor_send(value, axis, bit):
    size = lax.axis_size(axis)
    return lax.ppermute(value, axis, [(i, i ^ bit) for i in range(size)])


def halve(mine, axis, bit):
    rows = mine.shape[0] // 2
    upper = (lax.axis_index(axis) & bit) != 0
    kept = jnp.where(upper, mine[rows:], mine[:rows])
    sent = jnp.where(upper, mine[:rows], mine[rows:])
    return kept + xor_send(sent.astype(BF16), axis, bit).astype(F32)


def double(mine, axis, bit):
    upper = (lax.axis_index(axis) & bit) != 0
    other = xor_send(mine, axis, bit)
    return jnp.concatenate([jnp.where(upper, other, mine), jnp.where(upper, mine, other)], axis=0)


def bits_of(size):
    return [1 << i for i in range(size.bit_length() - 1)]


class Summed:
    def __init__(self, part, axis):
        bits = bits_of(lax.axis_size(axis))
        self.axis, self.part = axis, part
        self.steps = [(halve, bit) for bit in bits] + [(double, bit) for bit in reversed(bits)]
        self.doubling = len(bits)

    def step(self, *others):
        if not self.steps or (self.doubling == len(self.steps) and self.part.dtype != BF16):
            self.part = self.part.astype(BF16)
        if self.steps:
            run, bit = self.steps.pop(0)
            self.part = run(after(self.part, *others) if others else self.part, self.axis, bit)
        return self.part

    def rest(self, *others):
        while self.steps:
            self.step(*others)
            others = ()
        return self.part.astype(F32)


def one_hot(rows, columns):
    return (lax.broadcasted_iota(jnp.int32, (rows, columns.shape[0]), 0) == columns[None, :]).astype(BF16)


def dot(a, b):
    return jnp.dot(a, b, preferred_element_type=F32)


def chunk_widths(features, share):
    unit = 256
    if features % unit or features < 2 * unit:
        return [features]
    first = int(round(features * share / unit)) * unit
    return [first, features - first]


def on_device(routes, slots, gate, grad_out, saved_inputs, w_in, w_out, dense_partial):
    groups = lax.axis_size("expert")
    models = lax.axis_size("mp")
    me = lax.axis_index("mp")
    slot_rows = saved_inputs.shape[1]
    cap = slot_rows // groups
    tok_count, features = grad_out.shape
    pair = models == 2
    fold = 2 if pair and features % 512 == 0 else 1
    rows = fold * slot_rows

    scaled = (gate[:, None] * grad_out.astype(F32)).astype(BF16)
    columns = jnp.concatenate(
        [jnp.where(slots >= 0, routes * (fold * cap) + h * cap + slots, -1) for h in range(fold)]
    )
    table = one_hot(rows, columns)
    slot = jnp.arange(slot_rows, dtype=jnp.int32)
    spread = [one_hot(rows, (slot // cap) * (fold * cap) + h * cap + slot % cap) for h in range(fold)]

    widths = chunk_widths(features, 0.625) if pair else [features]
    starts = [sum(widths[:i]) for i in range(len(widths))]

    def all_to_all(block):
        wide = block.shape[1]
        block = block.reshape(groups, fold * cap, wide)
        return lax.all_to_all(block, "expert", split_axis=0, concat_axis=0, tiled=True).reshape(rows, wide)

    def nt_dot(a, b):
        return lax.dot_general(a, b, NT, preferred_element_type=F32)

    def tn_dot(a, b):
        return lax.dot_general(a, b, (((0,), (0,)), ((), ())), preferred_element_type=F32)

    outgoing = []
    for start, width in zip(starts, widths):
        part = width // fold
        stacked = jnp.concatenate(
            [scaled[:, start + h * part : start + (h + 1) * part] for h in range(fold)], axis=0
        )
        outgoing.append(dot(table, stacked).astype(BF16))

    dense = Summed(dense_partial[0], "expert")
    saved = saved_inputs[0]
    slopes = lax.optimization_barrier(slope_of(dot(saved, w_in[0])))
    arrived = [all_to_all(outgoing[0])]
    for block in outgoing[1:]:
        arrived.append(all_to_all(after(block, arrived[-1], slopes)))
    mine = [jnp.concatenate([tn_dot(t, block).astype(BF16) for t in spread], axis=1) for block in arrived]

    def up_share(who, i, x):
        w = lax.dynamic_slice_in_dim(w_out[0], who * features + starts[i], widths[i], 1)
        return nt_dot(x, w)

    if pair:
        theirs = [xor_send(own, "mp", 1) for own in mine]
        upstream = lax.optimization_barrier(up_share(me, 0, mine[0]))
        dense.step(slopes)
        for i in range(1, len(widths)):
            fence = dense.step(arrived[i])
            upstream = lax.optimization_barrier(upstream + up_share(1 - me, i - 1, after(theirs[i - 1], fence)))
            upstream = lax.optimization_barrier(upstream + up_share(me, i, mine[i]))
        upstream = upstream + up_share(1 - me, len(widths) - 1, theirs[-1])
    else:
        upstream = nt_dot(lax.all_gather(mine[0], "mp", axis=1, tiled=True), w_out[0])
    hidden = lax.optimization_barrier((upstream * slopes).astype(BF16))

    widths = chunk_widths(features, 0.625) if pair else [features]
    starts = [sum(widths[:i]) for i in range(len(widths))]
    order = list(reversed(range(len(widths))))

    def down_share(source, who, i):
        w = lax.dynamic_slice_in_dim(w_in[0], who * features + starts[i], widths[i], 0)
        return nt_dot(source, w)

    if pair:
        while len(dense.steps) > dense.doubling:
            dense.step()
        leaving = {}
        source = hidden
        for i in order:
            leaving[i] = lax.optimization_barrier(down_share(source, 1 - me, i).astype(BF16))
            source = after(hidden, leaving[i])
        for _ in range(dense.doubling // 2):
            dense.step(hidden)
    outs = {}
    last = None
    for i in order:
        part = widths[i] // fold
        if pair:
            sent = xor_send(leaving[i] if last is None else after(leaving[i], folded), "mp", 1)
            kept = lax.optimization_barrier(down_share(source, me, i))
            total = (kept + sent.astype(F32)).astype(BF16)
        else:
            total = lax.psum_scatter(
                nt_dot(hidden, w_in[0]), "mp", scatter_dimension=1, tiled=True
            ).astype(BF16)
        folded = sum(dot(t, total[:, h * part : (h + 1) * part]) for h, t in enumerate(spread)).astype(BF16)
        if pair:
            source = after(hidden, dense.step(folded))
        if last is not None:
            folded = after(folded, last)
        last = all_to_all(folded)
        outs[i] = jnp.concatenate(
            [tn_dot(table[:, h * tok_count : (h + 1) * tok_count], last).astype(BF16) for h in range(fold)],
            axis=1,
        )
    dense_sum = dense.rest()
    return (jnp.concatenate([outs[i] for i in sorted(order)], axis=1), dense_sum)


def solution(mesh):
    in_specs = (
        P("expert"),
        P("expert"),
        P("expert"),
        P("expert", "mp"),
        P("expert", None, None),
        P("expert", None, "mp"),
        P("expert", "mp", None),
        P("expert", None, "mp"),
    )
    out_specs = (P("expert", "mp"), P(None, "mp"))
    return jax.shard_map(
        on_device, mesh=mesh, in_specs=in_specs, out_specs=out_specs, check_vma=False
    )
```

```python
import math

import jax
import jax.numpy as jnp
from jax import lax
from jax.experimental import pallas as pl
from jax.experimental.pallas import tpu as pltpu
from jax.sharding import PartitionSpec as P

gelu_scale = math.sqrt(2.0 / math.pi)
cubic_coef = 0.044715
BF16 = jnp.bfloat16
F32 = jnp.float32
NT = (((1,), (1,)), ((), ()))


def slope_of(preact):
    inner = gelu_scale * (preact + cubic_coef * preact * preact * preact)
    tanh_val = jnp.tanh(inner)
    return 0.5 * (1.0 + tanh_val) + 0.5 * preact * (1.0 - tanh_val * tanh_val) * gelu_scale * (
        1.0 + 3.0 * cubic_coef * preact * preact
    )


def after(value, *others):
    return lax.optimization_barrier((value,) + others)[0]


def xor_send(value, axis, bit):
    size = lax.axis_size(axis)
    return lax.ppermute(value, axis, [(i, i ^ bit) for i in range(size)])


def halve(mine, axis, bit):
    rows = mine.shape[0] // 2
    upper = (lax.axis_index(axis) & bit) != 0
    kept = jnp.where(upper, mine[rows:], mine[:rows])
    sent = jnp.where(upper, mine[:rows], mine[rows:])
    return kept + xor_send(sent.astype(BF16), axis, bit).astype(F32)


def double(mine, axis, bit):
    upper = (lax.axis_index(axis) & bit) != 0
    other = xor_send(mine, axis, bit)
    return jnp.concatenate([jnp.where(upper, other, mine), jnp.where(upper, mine, other)], axis=0)


def bits_of(size):
    return [1 << i for i in range(size.bit_length() - 1)]


class Summed:
    def __init__(self, part, axis):
        bits = bits_of(lax.axis_size(axis))
        self.axis, self.part = axis, part
        self.steps = [(halve, bit) for bit in bits] + [(double, bit) for bit in reversed(bits)]
        self.doubling = len(bits)

    def step(self, *others):
        if not self.steps or (self.doubling == len(self.steps) and self.part.dtype != BF16):
            self.part = self.part.astype(BF16)
        if self.steps:
            run, bit = self.steps.pop(0)
            self.part = run(after(self.part, *others) if others else self.part, self.axis, bit)
        return self.part

    def rest(self, *others):
        while self.steps:
            self.step(*others)
            others = ()
        return self.part.astype(F32)


def one_hot(rows, columns):
    return (lax.broadcasted_iota(jnp.int32, (rows, columns.shape[0]), 0) == columns[None, :]).astype(BF16)


def dot(a, b):
    return jnp.dot(a, b, preferred_element_type=F32)


def column_of(row):
    return jnp.broadcast_to(row.astype(F32), (8, row.shape[1])).T[:, :1]


def spread_tokens(gate, columns, grad_out, width, rows):
    fold, tokens = columns.shape
    part, steps = width // fold, 2 if rows % 32 == 0 else 1
    block = rows // steps

    def kernel(gate_ref, columns_ref, grad_ref, out):
        scaled = (column_of(gate_ref[...]) * grad_ref[...].astype(F32)).astype(BF16)
        number = lax.broadcasted_iota(jnp.int32, (block, tokens), 0) + pl.program_id(0) * block
        total = None
        for h in range(fold):
            picked = jnp.where(number == columns_ref[h : h + 1, :], 1.0, 0.0).astype(BF16)
            term = jnp.dot(picked, scaled[:, h * part : (h + 1) * part], preferred_element_type=F32)
            total = term if total is None else total + term
        out[...] = total.astype(BF16)

    return pl.pallas_call(
        kernel,
        out_shape=jax.ShapeDtypeStruct((rows, part), BF16),
        grid=(steps,),
        in_specs=[
            pl.BlockSpec((1, tokens), lambda i: (0, 0)),
            pl.BlockSpec((fold, tokens), lambda i: (0, 0)),
            pl.BlockSpec((tokens, width), lambda i: (0, 0)),
        ],
        out_specs=pl.BlockSpec((block, part), lambda i: (i, 0)),
        compiler_params=pltpu.CompilerParams(vmem_limit_bytes=24 << 20),
    )(gate.reshape(1, tokens), columns, grad_out)


def gather_tokens(columns, block, tail):
    fold, tokens = columns.shape
    rows, part = block.shape
    steps = 2 if tokens % 256 == 0 else 1
    share = tokens // steps
    width = fold * part

    def kernel(columns_ref, block_ref, tail_ref, out):
        for h in range(fold):
            column = column_of(columns_ref[h : h + 1, :]).astype(jnp.int32)
            number = lax.broadcasted_iota(jnp.int32, (share, rows), 1)
            picked = jnp.where(number == column, 1.0, 0.0).astype(BF16)
            out[:, h * part : (h + 1) * part] = jnp.dot(
                picked, block_ref[...], preferred_element_type=F32
            ).astype(BF16)
        out[:, width:] = tail_ref[...]

    return pl.pallas_call(
        kernel,
        out_shape=jax.ShapeDtypeStruct((tokens, width + tail.shape[1]), BF16),
        grid=(steps,),
        in_specs=[
            pl.BlockSpec((fold, share), lambda i: (0, i)),
            pl.BlockSpec((rows, part), lambda i: (0, 0)),
            pl.BlockSpec((share, tail.shape[1]), lambda i: (i, 0)),
        ],
        out_specs=pl.BlockSpec((share, width + tail.shape[1]), lambda i: (i, 0)),
        compiler_params=pltpu.CompilerParams(vmem_limit_bytes=24 << 20),
    )(columns, block, tail)


def chunk_widths(features, share):
    unit = 256
    if features % unit or features < 2 * unit:
        return [features]
    first = int(round(features * share / unit)) * unit
    return [first, features - first]


def on_device(routes, slots, gate, grad_out, saved_inputs, w_in, w_out, dense_partial):
    groups = lax.axis_size("expert")
    models = lax.axis_size("mp")
    me = lax.axis_index("mp")
    slot_rows = saved_inputs.shape[1]
    cap = slot_rows // groups
    tok_count, features = grad_out.shape
    pair = models == 2
    fold = 2 if pair and features % 512 == 0 else 1
    rows = fold * slot_rows

    scaled = (gate[:, None] * grad_out.astype(F32)).astype(BF16)
    columns = jnp.concatenate(
        [jnp.where(slots >= 0, routes * (fold * cap) + h * cap + slots, -1) for h in range(fold)]
    )
    table = one_hot(rows, columns)
    slot = jnp.arange(slot_rows, dtype=jnp.int32)
    spread = [one_hot(rows, (slot // cap) * (fold * cap) + h * cap + slot % cap) for h in range(fold)]

    widths = chunk_widths(features, 0.625) if pair else [features]
    starts = [sum(widths[:i]) for i in range(len(widths))]

    def all_to_all(block):
        wide = block.shape[1]
        block = block.reshape(groups, fold * cap, wide)
        return lax.all_to_all(block, "expert", split_axis=0, concat_axis=0, tiled=True).reshape(rows, wide)

    def nt_dot(a, b):
        return lax.dot_general(a, b, NT, preferred_element_type=F32)

    def tn_dot(a, b):
        return lax.dot_general(a, b, (((0,), (0,)), ((), ())), preferred_element_type=F32)

    outgoing = []
    for start, width in zip(starts, widths):
        part = width // fold
        tokens = after(grad_out, *outgoing) if pair and outgoing else grad_out
        tokens = tokens[:, start : start + width].astype(F32)
        scaled = (gate[:, None] * tokens).astype(BF16)
        stacked = jnp.concatenate([scaled[:, h * part : (h + 1) * part] for h in range(fold)], axis=0)
        outgoing.append(dot(table, stacked).astype(BF16))

    dense = Summed(dense_partial[0], "expert")
    saved = saved_inputs[0]
    slopes = lax.optimization_barrier(slope_of(dot(saved, w_in[0])))
    arrived = [all_to_all(outgoing[0])]
    for block in outgoing[1:]:
        arrived.append(all_to_all(after(block, arrived[-1], slopes)))
    mine = [jnp.concatenate([tn_dot(t, block).astype(BF16) for t in spread], axis=1) for block in arrived]

    def up_share(who, i, x):
        w = lax.dynamic_slice_in_dim(w_out[0], who * features + starts[i], widths[i], 1)
        return nt_dot(x, w)

    if pair:
        theirs = [xor_send(own, "mp", 1) for own in mine]
        upstream = lax.optimization_barrier(up_share(me, 0, mine[0]))
        dense.step(slopes)
        for i in range(1, len(widths)):
            fence = dense.step(arrived[i])
            upstream = lax.optimization_barrier(upstream + up_share(1 - me, i - 1, after(theirs[i - 1], fence)))
            upstream = lax.optimization_barrier(upstream + up_share(me, i, mine[i]))
        upstream = upstream + up_share(1 - me, len(widths) - 1, theirs[-1])
    else:
        upstream = nt_dot(lax.all_gather(mine[0], "mp", axis=1, tiled=True), w_out[0])
    hidden = lax.optimization_barrier((upstream * slopes).astype(BF16))

    widths = chunk_widths(features, 0.625) if pair else [features]
    starts = [sum(widths[:i]) for i in range(len(widths))]
    order = list(reversed(range(len(widths))))

    def down_share(source, who, i):
        w = lax.dynamic_slice_in_dim(w_in[0], who * features + starts[i], widths[i], 0)
        return nt_dot(source, w)

    if pair:
        while len(dense.steps) > dense.doubling:
            dense.step()
        leaving = {}
        source = hidden
        for i in order:
            leaving[i] = lax.optimization_barrier(down_share(source, 1 - me, i).astype(BF16))
            source = after(hidden, leaving[i])
        for _ in range(dense.doubling // 2):
            dense.step(hidden)
    outs = {}
    last = None
    for i in order:
        part = widths[i] // fold
        if pair:
            sent = xor_send(leaving[i] if last is None else after(leaving[i], folded), "mp", 1)
            kept = lax.optimization_barrier(down_share(source, me, i))
            total = (kept + sent.astype(F32)).astype(BF16)
        else:
            total = lax.psum_scatter(
                nt_dot(hidden, w_in[0]), "mp", scatter_dimension=1, tiled=True
            ).astype(BF16)
        folded = sum(dot(t, total[:, h * part : (h + 1) * part]) for h, t in enumerate(spread)).astype(BF16)
        if pair:
            source = after(hidden, dense.step(folded))
        if last is not None:
            folded = after(folded, last)
        last = all_to_all(folded)
        if pair and not i and len(order) > 1:
            grad_in = gather_tokens(columns.reshape(fold, tok_count), last, outs[1])
            break
        outs[i] = jnp.concatenate(
            [tn_dot(table[:, h * tok_count : (h + 1) * tok_count], last).astype(BF16) for h in range(fold)],
            axis=1,
        )
    else:
        grad_in = jnp.concatenate([outs[i] for i in sorted(order)], axis=1)
    return (grad_in, dense.rest())


def solution(mesh):
    in_specs = (
        P("expert"),
        P("expert"),
        P("expert"),
        P("expert", "mp"),
        P("expert", None, None),
        P("expert", None, "mp"),
        P("expert", "mp", None),
        P("expert", None, "mp"),
    )
    out_specs = (P("expert", "mp"), P(None, "mp"))
    return jax.shard_map(
        on_device, mesh=mesh, in_specs=in_specs, out_specs=out_specs, check_vma=False
    )
```

```python
import math

import jax
import jax.numpy as jnp
from jax import lax
from jax.experimental import pallas as pl
from jax.experimental.pallas import tpu as pltpu
from jax.sharding import PartitionSpec as P

gelu_scale = math.sqrt(2.0 / math.pi)
cubic_coef = 0.044715
BF16 = jnp.bfloat16
F32 = jnp.float32
NT = (((1,), (1,)), ((), ()))


def slope_of(preact):
    inner = gelu_scale * (preact + cubic_coef * preact * preact * preact)
    tanh_val = jnp.tanh(inner)
    return 0.5 * (1.0 + tanh_val) + 0.5 * preact * (1.0 - tanh_val * tanh_val) * gelu_scale * (
        1.0 + 3.0 * cubic_coef * preact * preact
    )


def after(value, *others):
    return lax.optimization_barrier((value,) + others)[0]


def xor_send(value, axis, bit):
    size = lax.axis_size(axis)
    return lax.ppermute(value, axis, [(i, i ^ bit) for i in range(size)])


def halve(mine, axis, bit):
    rows = mine.shape[0] // 2
    upper = (lax.axis_index(axis) & bit) != 0
    kept = jnp.where(upper, mine[rows:], mine[:rows])
    sent = jnp.where(upper, mine[:rows], mine[rows:])
    return kept + xor_send(sent.astype(BF16), axis, bit).astype(F32)


def double(mine, axis, bit):
    upper = (lax.axis_index(axis) & bit) != 0
    other = xor_send(mine, axis, bit)
    return jnp.concatenate([jnp.where(upper, other, mine), jnp.where(upper, mine, other)], axis=0)


def bits_of(size):
    return [1 << i for i in range(size.bit_length() - 1)]


class Summed:
    def __init__(self, part, axis):
        bits = bits_of(lax.axis_size(axis))
        self.axis, self.part = axis, part
        self.steps = [(halve, bit) for bit in bits] + [(double, bit) for bit in reversed(bits)]
        self.doubling = len(bits)

    def step(self, *others):
        if not self.steps or (self.doubling == len(self.steps) and self.part.dtype != BF16):
            self.part = self.part.astype(BF16)
        if self.steps:
            run, bit = self.steps.pop(0)
            self.part = run(after(self.part, *others) if others else self.part, self.axis, bit)
        return self.part

    def rest(self, *others):
        while self.steps:
            self.step(*others)
            others = ()
        return self.part.astype(F32)


def one_hot(rows, columns):
    return (lax.broadcasted_iota(jnp.int32, (rows, columns.shape[0]), 0) == columns[None, :]).astype(BF16)


def dot(a, b):
    return jnp.dot(a, b, preferred_element_type=F32)


def column_of(row):
    return jnp.broadcast_to(row.astype(F32), (8, row.shape[1])).T[:, :1]


def spread_tokens(gate, columns, grad_out, width, rows):
    fold, tokens = columns.shape
    part, steps = width // fold, 2 if rows % 32 == 0 else 1
    block = rows // steps

    def kernel(gate_ref, columns_ref, grad_ref, out):
        scaled = (column_of(gate_ref[...]) * grad_ref[...].astype(F32)).astype(BF16)
        number = lax.broadcasted_iota(jnp.int32, (block, tokens), 0) + pl.program_id(0) * block
        total = None
        for h in range(fold):
            picked = jnp.where(number == columns_ref[h : h + 1, :], 1.0, 0.0).astype(BF16)
            term = jnp.dot(picked, scaled[:, h * part : (h + 1) * part], preferred_element_type=F32)
            total = term if total is None else total + term
        out[...] = total.astype(BF16)

    return pl.pallas_call(
        kernel,
        out_shape=jax.ShapeDtypeStruct((rows, part), BF16),
        grid=(steps,),
        in_specs=[
            pl.BlockSpec((1, tokens), lambda i: (0, 0)),
            pl.BlockSpec((fold, tokens), lambda i: (0, 0)),
            pl.BlockSpec((tokens, width), lambda i: (0, 0)),
        ],
        out_specs=pl.BlockSpec((block, part), lambda i: (i, 0)),
        compiler_params=pltpu.CompilerParams(vmem_limit_bytes=24 << 20),
    )(gate.reshape(1, tokens), columns, grad_out)


def gather_tokens(columns, block, tail):
    fold, tokens = columns.shape
    rows, part = block.shape
    steps = 2 if tokens % 256 == 0 else 1
    share = tokens // steps
    width = fold * part

    def kernel(columns_ref, block_ref, tail_ref, out):
        for h in range(fold):
            column = column_of(columns_ref[h : h + 1, :]).astype(jnp.int32)
            number = lax.broadcasted_iota(jnp.int32, (share, rows), 1)
            picked = jnp.where(number == column, 1.0, 0.0).astype(BF16)
            out[:, h * part : (h + 1) * part] = jnp.dot(
                picked, block_ref[...], preferred_element_type=F32
            ).astype(BF16)
        out[:, width:] = tail_ref[...]

    return pl.pallas_call(
        kernel,
        out_shape=jax.ShapeDtypeStruct((tokens, width + tail.shape[1]), BF16),
        grid=(steps,),
        in_specs=[
            pl.BlockSpec((fold, share), lambda i: (0, i)),
            pl.BlockSpec((rows, part), lambda i: (0, 0)),
            pl.BlockSpec((share, tail.shape[1]), lambda i: (i, 0)),
        ],
        out_specs=pl.BlockSpec((share, width + tail.shape[1]), lambda i: (i, 0)),
        compiler_params=pltpu.CompilerParams(vmem_limit_bytes=24 << 20),
    )(columns, block, tail)


def chunk_widths(features, share):
    unit = 256
    if features % unit or features < 2 * unit:
        return [features]
    first = int(round(features * share / unit)) * unit
    return [first, features - first]


def on_device(routes, slots, gate, grad_out, saved_inputs, w_in, w_out, dense_partial):
    groups = lax.axis_size("expert")
    models = lax.axis_size("mp")
    me = lax.axis_index("mp")
    slot_rows = saved_inputs.shape[1]
    cap = slot_rows // groups
    tok_count, features = grad_out.shape
    pair = models == 2
    fold = 2 if pair and features % 512 == 0 else 1
    rows = fold * slot_rows

    scaled = (gate[:, None] * grad_out.astype(F32)).astype(BF16)
    columns = jnp.concatenate(
        [jnp.where(slots >= 0, routes * (fold * cap) + h * cap + slots, -1) for h in range(fold)]
    )
    table = one_hot(rows, columns)
    slot = jnp.arange(slot_rows, dtype=jnp.int32)
    spread = [one_hot(rows, (slot // cap) * (fold * cap) + h * cap + slot % cap) for h in range(fold)]

    widths = chunk_widths(features, 0.625) if pair else [features]
    starts = [sum(widths[:i]) for i in range(len(widths))]

    def all_to_all(block):
        wide = block.shape[1]
        block = block.reshape(groups, fold * cap, wide)
        return lax.all_to_all(block, "expert", split_axis=0, concat_axis=0, tiled=True).reshape(rows, wide)

    def nt_dot(a, b):
        return lax.dot_general(a, b, NT, preferred_element_type=F32)

    def tn_dot(a, b):
        return lax.dot_general(a, b, (((0,), (0,)), ((), ())), preferred_element_type=F32)

    outgoing = []
    for start, width in zip(starts, widths):
        part = width // fold
        tokens = after(grad_out, *outgoing) if pair and outgoing else grad_out
        tokens = tokens[:, start : start + width].astype(F32)
        scaled = (gate[:, None] * tokens).astype(BF16)
        stacked = jnp.concatenate([scaled[:, h * part : (h + 1) * part] for h in range(fold)], axis=0)
        outgoing.append(dot(table, stacked).astype(BF16))

    dense = Summed(dense_partial[0], "expert")
    saved = saved_inputs[0]
    slopes = lax.optimization_barrier(slope_of(dot(saved, w_in[0])).astype(BF16))
    arrived = [all_to_all(outgoing[0])]
    for block in outgoing[1:]:
        arrived.append(all_to_all(after(block, arrived[-1], slopes)))

    def unfolded(block):
        return jnp.concatenate([tn_dot(t, block).astype(BF16) for t in spread], axis=1)

    mine = [unfolded(block) for block in arrived]

    def up_share(who, i, x):
        w = lax.dynamic_slice_in_dim(w_out[0], who * features + starts[i], widths[i], 1)
        return nt_dot(x, w)

    if pair:
        theirs = [unfolded(xor_send(block, "mp", 1)) for block in arrived]
        upstream = lax.optimization_barrier(up_share(me, 0, mine[0]))
        dense.step(slopes)
        for i in range(1, len(widths)):
            fence = dense.step(arrived[i])
            upstream = lax.optimization_barrier(upstream + up_share(1 - me, i - 1, after(theirs[i - 1], fence)))
            upstream = lax.optimization_barrier(upstream + up_share(me, i, mine[i]))
        upstream = upstream + up_share(1 - me, len(widths) - 1, theirs[-1])
    else:
        upstream = nt_dot(lax.all_gather(mine[0], "mp", axis=1, tiled=True), w_out[0])
    hidden = lax.optimization_barrier((upstream * slopes.astype(F32)).astype(BF16))

    widths = chunk_widths(features, 0.625) if pair else [features]
    starts = [sum(widths[:i]) for i in range(len(widths))]
    order = list(reversed(range(len(widths))))

    def down_share(source, who, i):
        w = lax.dynamic_slice_in_dim(w_in[0], who * features + starts[i], widths[i], 0)
        return nt_dot(source, w)

    if pair:
        while len(dense.steps) > dense.doubling:
            dense.step()
        leaving = {}
        source = hidden
        for i in order:
            leaving[i] = lax.optimization_barrier(down_share(source, 1 - me, i).astype(BF16))
            source = after(hidden, leaving[i])
        for _ in range(dense.doubling // 2):
            dense.step(hidden)
    outs = {}
    last = None
    for i in order:
        part = widths[i] // fold
        if pair:
            sent = xor_send(leaving[i] if last is None else after(leaving[i], folded), "mp", 1)
            kept = lax.optimization_barrier(down_share(source, me, i))
            total = (kept + sent.astype(F32)).astype(BF16)
        else:
            total = lax.psum_scatter(
                nt_dot(hidden, w_in[0]), "mp", scatter_dimension=1, tiled=True
            ).astype(BF16)
        folded = sum(dot(t, total[:, h * part : (h + 1) * part]) for h, t in enumerate(spread)).astype(BF16)
        if pair:
            source = after(hidden, dense.step(folded))
        if last is not None:
            folded = after(folded, last)
        last = all_to_all(folded)
        if pair and not i and len(order) > 1:
            grad_in = gather_tokens(columns.reshape(fold, tok_count), last, outs[1])
            break
        outs[i] = jnp.concatenate(
            [tn_dot(table[:, h * tok_count : (h + 1) * tok_count], last).astype(BF16) for h in range(fold)],
            axis=1,
        )
    else:
        grad_in = jnp.concatenate([outs[i] for i in sorted(order)], axis=1)
    return (grad_in, dense.rest())


def solution(mesh):
    in_specs = (
        P("expert"),
        P("expert"),
        P("expert"),
        P("expert", "mp"),
        P("expert", None, None),
        P("expert", None, "mp"),
        P("expert", "mp", None),
        P("expert", None, "mp"),
    )
    out_specs = (P("expert", "mp"), P(None, "mp"))
    return jax.shard_map(
        on_device, mesh=mesh, in_specs=in_specs, out_specs=out_specs, check_vma=False
    )
```

```python
import math

import jax
import jax.numpy as jnp
from jax import lax
from jax.experimental import pallas as pl
from jax.experimental.pallas import tpu as pltpu
from jax.sharding import PartitionSpec as P

gelu_scale = math.sqrt(2.0 / math.pi)
cubic_coef = 0.044715
BF16 = jnp.bfloat16
F32 = jnp.float32
NT = (((1,), (1,)), ((), ()))


def slope_of(preact):
    inner = gelu_scale * (preact + cubic_coef * preact * preact * preact)
    tanh_val = jnp.tanh(inner)
    return 0.5 * (1.0 + tanh_val) + 0.5 * preact * (1.0 - tanh_val * tanh_val) * gelu_scale * (
        1.0 + 3.0 * cubic_coef * preact * preact
    )


def after(value, *others):
    return lax.optimization_barrier((value,) + others)[0]


def xor_send(value, axis, bit):
    size = lax.axis_size(axis)
    return lax.ppermute(value, axis, [(i, i ^ bit) for i in range(size)])


def halve(mine, axis, bit):
    rows = mine.shape[0] // 2
    upper = (lax.axis_index(axis) & bit) != 0
    kept = jnp.where(upper, mine[rows:], mine[:rows])
    sent = jnp.where(upper, mine[:rows], mine[rows:])
    return kept + xor_send(sent.astype(BF16), axis, bit).astype(F32)


def double(mine, axis, bit):
    upper = (lax.axis_index(axis) & bit) != 0
    other = xor_send(mine, axis, bit)
    return jnp.concatenate([jnp.where(upper, other, mine), jnp.where(upper, mine, other)], axis=0)


def bits_of(size):
    return [1 << i for i in range(size.bit_length() - 1)]


class Summed:
    def __init__(self, part, axis):
        bits = bits_of(lax.axis_size(axis))
        self.axis, self.part = axis, part
        self.steps = [(halve, bit) for bit in bits] + [(double, bit) for bit in reversed(bits)]
        self.doubling = len(bits)

    def step(self, *others):
        if not self.steps or (self.doubling == len(self.steps) and self.part.dtype != BF16):
            self.part = self.part.astype(BF16)
        if self.steps:
            run, bit = self.steps.pop(0)
            self.part = run(after(self.part, *others) if others else self.part, self.axis, bit)
        return self.part

    def rest(self, *others):
        while self.steps:
            self.step(*others)
            others = ()
        return self.part.astype(F32)


def one_hot(rows, columns):
    return (lax.broadcasted_iota(jnp.int32, (rows, columns.shape[0]), 0) == columns[None, :]).astype(BF16)


def dot(a, b):
    return jnp.dot(a, b, preferred_element_type=F32)


def column_of(row):
    return jnp.broadcast_to(row.astype(F32), (8, row.shape[1])).T[:, :1]


def spread_tokens(gate, columns, grad_out, width, rows):
    fold, tokens = columns.shape
    part, steps = width // fold, 2 if rows % 32 == 0 else 1
    block = rows // steps

    def kernel(gate_ref, columns_ref, grad_ref, out):
        scaled = (column_of(gate_ref[...]) * grad_ref[...].astype(F32)).astype(BF16)
        number = lax.broadcasted_iota(jnp.int32, (block, tokens), 0) + pl.program_id(0) * block
        total = None
        for h in range(fold):
            picked = jnp.where(number == columns_ref[h : h + 1, :], 1.0, 0.0).astype(BF16)
            term = jnp.dot(picked, scaled[:, h * part : (h + 1) * part], preferred_element_type=F32)
            total = term if total is None else total + term
        out[...] = total.astype(BF16)

    return pl.pallas_call(
        kernel,
        out_shape=jax.ShapeDtypeStruct((rows, part), BF16),
        grid=(steps,),
        in_specs=[
            pl.BlockSpec((1, tokens), lambda i: (0, 0)),
            pl.BlockSpec((fold, tokens), lambda i: (0, 0)),
            pl.BlockSpec((tokens, width), lambda i: (0, 0)),
        ],
        out_specs=pl.BlockSpec((block, part), lambda i: (i, 0)),
        compiler_params=pltpu.CompilerParams(vmem_limit_bytes=24 << 20),
    )(gate.reshape(1, tokens), columns, grad_out)


def gather_tokens(columns, block, tail):
    fold, tokens = columns.shape
    rows, part = block.shape
    steps = 2 if tokens % 256 == 0 else 1
    share = tokens // steps
    width = fold * part

    def kernel(columns_ref, block_ref, tail_ref, out):
        for h in range(fold):
            column = column_of(columns_ref[h : h + 1, :]).astype(jnp.int32)
            number = lax.broadcasted_iota(jnp.int32, (share, rows), 1)
            picked = jnp.where(number == column, 1.0, 0.0).astype(BF16)
            out[:, h * part : (h + 1) * part] = jnp.dot(
                picked, block_ref[...], preferred_element_type=F32
            ).astype(BF16)
        out[:, width:] = tail_ref[...]

    return pl.pallas_call(
        kernel,
        out_shape=jax.ShapeDtypeStruct((tokens, width + tail.shape[1]), BF16),
        grid=(steps,),
        in_specs=[
            pl.BlockSpec((fold, share), lambda i: (0, i)),
            pl.BlockSpec((rows, part), lambda i: (0, 0)),
            pl.BlockSpec((share, tail.shape[1]), lambda i: (i, 0)),
        ],
        out_specs=pl.BlockSpec((share, width + tail.shape[1]), lambda i: (i, 0)),
        compiler_params=pltpu.CompilerParams(vmem_limit_bytes=24 << 20),
    )(columns, block, tail)


def chunk_widths(features, share):
    unit = 256
    if features % unit or features < 2 * unit:
        return [features]
    first = int(round(features * share / unit)) * unit
    return [first, features - first]


def on_device(routes, slots, gate, grad_out, saved_inputs, w_in, w_out, dense_partial):
    groups = lax.axis_size("expert")
    models = lax.axis_size("mp")
    me = lax.axis_index("mp")
    slot_rows = saved_inputs.shape[1]
    cap = slot_rows // groups
    tok_count, features = grad_out.shape
    pair = models == 2
    fold = 2 if pair and features % 512 == 0 else 1
    rows = fold * slot_rows

    scaled = (gate[:, None] * grad_out.astype(F32)).astype(BF16)
    columns = jnp.concatenate(
        [jnp.where(slots >= 0, routes * (fold * cap) + h * cap + slots, -1) for h in range(fold)]
    )
    table = one_hot(rows, columns)
    slot = jnp.arange(slot_rows, dtype=jnp.int32)
    spread = [one_hot(rows, (slot // cap) * (fold * cap) + h * cap + slot % cap) for h in range(fold)]

    widths = chunk_widths(features, 0.625) if pair else [features]
    starts = [sum(widths[:i]) for i in range(len(widths))]

    def all_to_all(block):
        wide = block.shape[1]
        block = block.reshape(groups, fold * cap, wide)
        return lax.all_to_all(block, "expert", split_axis=0, concat_axis=0, tiled=True).reshape(rows, wide)

    def nt_dot(a, b):
        return lax.dot_general(a, b, NT, preferred_element_type=F32)

    def tn_dot(a, b):
        return lax.dot_general(a, b, (((0,), (0,)), ((), ())), preferred_element_type=F32)

    outgoing = []
    for start, width in zip(starts, widths):
        part = width // fold
        tokens = after(grad_out, *outgoing) if pair and outgoing else grad_out
        tokens = tokens[:, start : start + width].astype(F32)
        scaled = (gate[:, None] * tokens).astype(BF16)
        stacked = jnp.concatenate([scaled[:, h * part : (h + 1) * part] for h in range(fold)], axis=0)
        outgoing.append(dot(table, stacked).astype(BF16))

    dense = Summed(dense_partial[0], "expert")
    saved = saved_inputs[0]
    slopes = lax.optimization_barrier(slope_of(dot(saved, w_in[0])))
    arrived = [all_to_all(outgoing[0])]
    for block in outgoing[1:]:
        arrived.append(all_to_all(after(block, arrived[-1], slopes)))

    def unfolded(block):
        return jnp.concatenate([tn_dot(t, block).astype(BF16) for t in spread], axis=1)

    mine = [unfolded(block) for block in arrived]

    def up_share(who, i, x):
        w = lax.dynamic_slice_in_dim(w_out[0], who * features + starts[i], widths[i], 1)
        return nt_dot(x, w)

    if pair:
        theirs = [unfolded(xor_send(block, "mp", 1)) for block in arrived]
        upstream = lax.optimization_barrier(up_share(me, 0, mine[0]))
        dense.step(slopes)
        for i in range(1, len(widths)):
            fence = dense.step(arrived[i])
            upstream = lax.optimization_barrier(upstream + up_share(1 - me, i - 1, after(theirs[i - 1], fence)))
            upstream = lax.optimization_barrier(upstream + up_share(me, i, mine[i]))
        upstream = upstream + up_share(1 - me, len(widths) - 1, theirs[-1])
    else:
        upstream = nt_dot(lax.all_gather(mine[0], "mp", axis=1, tiled=True), w_out[0])
    hidden = lax.optimization_barrier((upstream * slopes).astype(BF16))

    widths = chunk_widths(features, 0.625) if pair else [features]
    starts = [sum(widths[:i]) for i in range(len(widths))]
    order = list(reversed(range(len(widths))))

    def down_share(source, who, i):
        w = lax.dynamic_slice_in_dim(w_in[0], who * features + starts[i], widths[i], 0)
        return nt_dot(source, w)

    if pair:
        while len(dense.steps) > dense.doubling:
            dense.step()
        leaving = {}
        source = hidden
        for i in order:
            leaving[i] = lax.optimization_barrier(down_share(source, 1 - me, i).astype(BF16))
            source = after(hidden, leaving[i])
        for _ in range(dense.doubling // 2):
            dense.step(hidden)
    outs = {}
    last = None
    for i in order:
        part = widths[i] // fold
        if pair:
            sent = xor_send(leaving[i] if last is None else after(leaving[i], folded), "mp", 1)
            kept = lax.optimization_barrier(down_share(source, me, i))
            total = (kept + sent.astype(F32)).astype(BF16)
        else:
            total = lax.psum_scatter(
                nt_dot(hidden, w_in[0]), "mp", scatter_dimension=1, tiled=True
            ).astype(BF16)
        folded = sum(dot(t, total[:, h * part : (h + 1) * part]) for h, t in enumerate(spread)).astype(BF16)
        if pair:
            source = after(hidden, dense.step(folded))
        if last is not None:
            folded = after(folded, last)
        last = all_to_all(folded)
        if pair and not i and len(order) > 1:
            grad_in = gather_tokens(columns.reshape(fold, tok_count), last, outs[1])
            break
        outs[i] = jnp.concatenate(
            [tn_dot(table[:, h * tok_count : (h + 1) * tok_count], last).astype(BF16) for h in range(fold)],
            axis=1,
        )
    else:
        grad_in = jnp.concatenate([outs[i] for i in sorted(order)], axis=1)
    return (grad_in, dense.rest())


def solution(mesh):
    in_specs = (
        P("expert"),
        P("expert"),
        P("expert"),
        P("expert", "mp"),
        P("expert", None, None),
        P("expert", None, "mp"),
        P("expert", "mp", None),
        P("expert", None, "mp"),
    )
    out_specs = (P("expert", "mp"), P(None, "mp"))
    return jax.shard_map(
        on_device, mesh=mesh, in_specs=in_specs, out_specs=out_specs, check_vma=False
    )
```
